32 devices in a mesh: member: 2 (over y), tile: 4 (over z), face: 4 (over x, core).
Axes of the slice: x: 2, y: 2, z: 4, core: 2. Of those that a mesh axis runs over, the one named last changes fastest.
Arguments:
- atmosphere: float32 [6, 4, 16, 32, 32], P('member', 'face', None, 'tile'), parts along dimension 0, may hold values from -6 to 6
- weight_in: bfloat16 [3, 3, 90, 16], replicated, may hold values from -0.5 to 0.5
- weight_block: bfloat16 [3, 3, 90, 90], replicated, may hold values from -0.21875 to 0.21875
- weight_mix: bfloat16 [90, 90], replicated, may hold values from -0.625 to 0.625
- weight_down: bfloat16 [3, 3, 180, 90], replicated, may hold values from -0.21875 to 0.21875
- weight_coarse: bfloat16 [3, 3, 180, 180], replicated, may hold values from -0.15625 to 0.15625
- weight_decode: bfloat16 [3, 3, 90, 270], replicated, may hold values from -0.125 to 0.125
- readout_matrix: bfloat16 [16, 90], replicated, may hold values from -0.625 to 0.625
Outputs:
- advanced_state: float32 [6, 4, 16, 32, 32], P('member', 'face', None, 'tile'), parts along dimension 0
The draws below stay inside these ranges and needn't reach their ends.
There are 2 independent parts, one for each index of `member`. The reference program is written for one: setup_inputs(seed, part) draws one part's arguments, and reference() takes and returns one part's arrays. A program takes and returns all parts, laid end to end along the dimension named above; an argument that names none is the same for every part. Nothing has to cross between parts.
All inputs are finite; a program needn't handle non-finite values.
Results may differ from the reference program's by a relative error of at most 0.0021.
Values may be sent and summed in bfloat16 or wider, within the bound.
A program may use at most 128 MiB of HBM per device.

```python
import jax
import jax.numpy as jnp
from jax import lax

F = 16
C0 = 90
C1 = 180
NSIDE = 32


def block_levels(stream_key, extent, pieces, low, top_value):
    def one(axis_at, parts):
        draws = jax.random.uniform(jax.random.fold_in(jax.random.fold_in(stream_key, 6), axis_at), (parts,), jnp.float32, low / len(pieces), top_value / len(pieces))
        return jnp.repeat(jnp.exp(draws), extent[axis_at] // parts).reshape((-1,) + (1,) * (len(extent) - axis_at - 1))

    factor_of = one(*pieces[0])
    for cut in pieces[1:]:
        factor_of = factor_of * one(*cut)
    return factor_of


def gaussian(key, dims, scale, most, shards=(), kind=jnp.bfloat16):
    loudness = block_levels(key, dims, shards, -0.22, 0.18) if shards else 1.0
    drawn = jax.random.normal(key, dims, jnp.float32) * scale * loudness
    return jnp.minimum(jnp.maximum(drawn, -most), most).astype(kind)


def setup_inputs(seed: int = 0, part: int = 0) -> dict:
    keys = jax.random.split(jax.random.key(seed), 9)
    part_keys = jax.random.split(jax.random.fold_in(keys[8], part), 9)
    return {
        "atmosphere": gaussian(part_keys[0], (3, 4, F, NSIDE, NSIDE), 1.0, 6.0, ((1, 4), (3, 4)), jnp.float32),
        "weight_in": gaussian(keys[1], (3, 3, C0, F), (9 * F) ** -0.5, 0.5),
        "weight_block": gaussian(keys[2], (3, 3, C0, C0), (9 * C0) ** -0.5, 0.21875),
        "weight_mix": gaussian(keys[3], (C0, C0), C0 ** -0.5, 0.625),
        "weight_down": gaussian(keys[4], (3, 3, C1, C0), (9 * C0) ** -0.5, 0.21875),
        "weight_coarse": gaussian(keys[5], (3, 3, C1, C1), (9 * C1) ** -0.5, 0.15625),
        "weight_decode": gaussian(keys[6], (3, 3, C0, C0 + C1), (9 * (C0 + C1)) ** -0.5, 0.125),
        "readout_matrix": gaussian(keys[7], (F, C0), C0 ** -0.5, 0.625),
    }


def rolled_next(stacked):
    return jnp.roll(stacked, -1, axis=0)


def rolled_prev(stacked):
    return jnp.roll(stacked, 1, axis=0)


def pad_sphere(values, halo_width):
    north_face, equator, south_face = values[0], values[1], values[2]
    face_size = values.shape[-1]
    rim_start = face_size - halo_width
    top_rows = jnp.stack([jnp.flip(jnp.swapaxes(rolled_next(north_face)[..., :halo_width], -1, -2), -2), north_face[..., rim_start:, :], equator[..., rim_start:, :]])
    bottom = jnp.stack([equator[..., :halo_width, :], south_face[..., :halo_width, :], jnp.flip(jnp.swapaxes(rolled_next(south_face)[..., rim_start:], -1, -2), -2)])
    left_cols = jnp.stack([jnp.flip(jnp.swapaxes(rolled_prev(north_face)[..., :halo_width, :], -1, -2), -1), rolled_prev(north_face)[..., rim_start:], rolled_prev(equator)[..., rim_start:]])
    right_cols = jnp.stack([rolled_next(equator)[..., :halo_width], rolled_next(south_face)[..., :halo_width], jnp.flip(jnp.swapaxes(rolled_prev(south_face)[..., rim_start:, :], -1, -2), -1)])
    corner = jnp.zeros(values.shape[:-2] + (halo_width, halo_width), values.dtype)
    middle = jnp.concatenate([left_cols, values, right_cols], -1)
    upper_rows = jnp.concatenate([corner, top_rows, corner], -1)
    lower_rows = jnp.concatenate([corner, bottom, corner], -1)
    return jnp.concatenate([upper_rows, middle, lower_rows], -2)


def convolve(padded, weight, dilation):
    out_size = padded.shape[-1] - 2 * dilation
    flattened = padded.reshape((12,) + padded.shape[2:])

    def one_face(panel_values):
        summed = jnp.zeros((weight.shape[2], out_size, out_size), jnp.float32)
        for row_tap in range(3):
            for col_tap in range(3):
                window_patch = panel_values[:, row_tap * dilation:row_tap * dilation + out_size, col_tap * dilation:col_tap * dilation + out_size]
                summed = summed + jnp.einsum("oc,crn->orn", weight[row_tap, col_tap].astype(jnp.float32), window_patch.astype(jnp.float32))
        return summed

    result = lax.map(one_face, flattened)
    return result.reshape((3, 4) + result.shape[1:])


def pool_cells(values):
    shape = values.shape
    wide = values.astype(jnp.float32).reshape(shape[:-2] + (shape[-2] // 2, 2, shape[-1] // 2, 2))
    return jnp.mean(wide, axis=(-3, -1))


def upsample(values):
    shape = values.shape
    grown = jnp.broadcast_to(values[..., :, None, :, None], shape[:-2] + (shape[-2], 2, shape[-1], 2))
    return grown.reshape(shape[:-2] + (2 * shape[-2], 2 * shape[-1]))


def per_cell_channel_blend(weight, values):
    return jnp.einsum("oc,fgcrn->fgorn", weight.astype(jnp.float32), values.astype(jnp.float32))


def reference(atmosphere, weight_in, weight_block, weight_mix, weight_down, weight_coarse, weight_decode, readout_matrix):
    source = atmosphere.astype(jnp.bfloat16)
    encoded = jax.nn.gelu(convolve(pad_sphere(source, 1), weight_in, 1)).astype(jnp.bfloat16)
    inner_out = jax.nn.gelu(convolve(pad_sphere(encoded, 1), weight_block, 1)).astype(jnp.bfloat16)
    skip_level = (encoded.astype(jnp.float32) + per_cell_channel_blend(weight_mix, inner_out)).astype(jnp.bfloat16)
    pooled = pool_cells(skip_level).astype(jnp.bfloat16)
    coarse_one = jax.nn.gelu(convolve(pad_sphere(pooled, 2), weight_down, 2)).astype(jnp.bfloat16)
    coarse_two = (coarse_one.astype(jnp.float32) + jax.nn.gelu(convolve(pad_sphere(coarse_one, 1), weight_coarse, 1))).astype(jnp.bfloat16)
    joined_features = jnp.concatenate([upsample(coarse_two), skip_level], 2)
    upscaled_activations = jax.nn.gelu(convolve(pad_sphere(joined_features, 1), weight_decode, 1)).astype(jnp.bfloat16)
    return atmosphere + per_cell_channel_blend(readout_matrix, upscaled_activations)
```

```python
import functools

import jax
import jax.numpy as jnp
from jax import lax
from jax.experimental import pallas as pl
from jax.experimental.pallas import tpu as pltpu
from jax.sharding import PartitionSpec as P

LANES = 128
EDGE = 8
F32 = jnp.float32
BF16 = jnp.bfloat16


def groups_of(channels):
    return -(-channels // LANES)


class Halo:
    def __init__(self, refs, rows, cols, width, groups, tiles):
        self.rows, self.cols, self.width = rows, cols, width
        self.groups, self.tiles = groups, tiles
        (self.x, self.sa, self.sb, self.sc, self.sd, self.se, self.sf, self.ra, self.rb,
         self.ru, self.rd, self.pc, self.pd, self.pe, self.pf, self.send, self.recv) = refs

    @staticmethod
    def shapes(rows, cols, width, groups, tiles):
        grid = (groups, 3, rows + 2 * width, cols + 2 * EDGE, LANES)
        pair = (groups, 2, width, rows, LANES)
        single = (groups, width, rows, LANES)
        long = (groups, width, rows + 2 * width, LANES)
        strip = (groups, 3, width, cols, LANES)
        count = 10 + 2 * tiles
        shapes = [grid, pair, pair, single, single, (tiles,) + long, (tiles,) + long,
                  (3,) + pair, (3,) + pair, strip, strip,
                  (tiles,) + single, (tiles,) + single, long, long]
        return [pltpu.VMEM(s, F32) for s in shapes] + [
            pltpu.SemaphoreType.DMA((count,)),
            pltpu.SemaphoreType.DMA((count,)),
        ]

    def copy(self, src, dst, send, recv, tile, face):
        return pltpu.make_async_remote_copy(
            src_ref=src, dst_ref=dst, send_sem=self.send.at[send], recv_sem=self.recv.at[recv],
            device_id={"tile": tile, "face": face}, device_id_type=pl.DeviceIdType.MESH)

    def copies(self, *names):
        tiles, w, rows, cols = self.tiles, self.width, self.rows, self.cols
        t, g = lax.axis_index("tile"), lax.axis_index("face")
        faces = lax.axis_size("face")
        west, east = lax.rem(g + faces - 1, faces), lax.rem(g + 1, faces)
        inner = pl.ds(EDGE, cols)
        found = []
        for name in names:
            if name == "common":
                for step in range(3):
                    to = lax.rem(t + tiles + step - 1, tiles)
                    found.append(self.copy(self.sa, self.ra.at[step], step, step, to, west))
                    found.append(self.copy(self.sb, self.rb.at[step], 3 + step, 3 + step, to, east))
                up, down = lax.rem(t + tiles - 1, tiles), lax.rem(t + 1, tiles)
                found.append(self.copy(self.x.at[:, :, pl.ds(w, w), inner, :], self.rd, 6, 6, up, g))
                found.append(self.copy(self.x.at[:, :, pl.ds(rows, w), inner, :], self.ru, 7, 7, down, g))
            elif name == "to_top":
                found.append(self.copy(self.sc, self.pc.at[t], 8, 10 + t, 0, west))
            elif name == "to_bottom":
                found.append(self.copy(self.sd, self.pd.at[t], 9, 10 + tiles + t, tiles - 1, west))
            for i in range(tiles):
                if name == "from_top":
                    found.append(self.copy(self.se.at[i], self.pe, 10 + i, 8, i, east))
                elif name == "from_bottom":
                    found.append(self.copy(self.sf.at[i], self.pf, 10 + tiles + i, 9, i, east))
                elif name == "at_top":
                    found.append(self.copy(self.sc, self.pc.at[i], 8, 10 + i, 0, west))
                elif name == "at_bottom":
                    found.append(self.copy(self.sd, self.pd.at[i], 9, 10 + tiles + i, 0, west))
        return found

    def start(self):
        tiles, w, rows, cols, x = self.tiles, self.width, self.rows, self.cols, self.x
        t = lax.axis_index("tile")
        for q in range(self.groups):
            for k in range(w):
                own = pl.ds(w, rows)
                first, last = EDGE + k, EDGE + cols - 1 - k
                self.sa[q, 0, k] = x[q, 1, own, first, :]
                self.sa[q, 1, k] = x[q, 2, own, first, :]
                self.sb[q, 0, k] = x[q, 0, own, last, :]
                self.sb[q, 1, k] = x[q, 1, own, last, :]
                self.sc[q, k] = x[q, 0, own, first, :]
                self.sd[q, k] = x[q, 2, own, last, :]
        for c in self.copies("common", "to_top", "to_bottom"):
            c.start()

        @pl.when(t == 0)
        def _():
            for i, c in enumerate(self.copies("from_top")):
                for q in range(self.groups):
                    for k in range(w):
                        self.se[i, q, k] = x[q, 0, w + k, pl.ds(EDGE + i * rows - w, rows + 2 * w), :]
                c.start()

        @pl.when(t == tiles - 1)
        def _():
            for i, c in enumerate(self.copies("from_bottom")):
                for q in range(self.groups):
                    for k in range(w):
                        self.sf[i, q, k] = x[
                            q, 2, w + rows - 1 - k, pl.ds(EDGE + i * rows - w, rows + 2 * w), :]
                c.start()

    def finish(self):
        tiles, w, rows, cols, x = self.tiles, self.width, self.rows, self.cols, self.x
        t = lax.axis_index("tile")
        for c in self.copies("common"):
            c.wait_recv()
        self.copy(self.se.at[0], self.pe, 10, 8, 0, 0).wait_recv()
        self.copy(self.sf.at[0], self.pf, 10, 9, 0, 0).wait_recv()
        for q in range(self.groups):
            for k in range(w):
                left, right = EDGE - 1 - k, EDGE + cols + k
                for f in range(2):
                    for face, col, got in ((1 + f, left, self.rb), (f, right, self.ra)):
                        x[q, face, pl.ds(w, rows), col, :] = got[1, q, f, k]
                        x[q, face, pl.ds(0, w), col, :] = got[2, q, f, k, pl.ds(rows - w, w), :]
                        x[q, face, pl.ds(w + rows, w), col, :] = got[0, q, f, k, pl.ds(0, w), :]
                x[q, 0, :, left, :] = self.pe[q, k]
                x[q, 2, :, right, :] = self.pf[q, k]
        for q in range(self.groups):
            for f in range(3):
                x[q, f, pl.ds(0, w), pl.ds(EDGE, cols), :] = self.ru[q, f]
                x[q, f, pl.ds(w + rows, w), pl.ds(EDGE, cols), :] = self.rd[q, f]
        blank = jnp.zeros((w, EDGE, LANES), F32)

        @pl.when(t == 0)
        def _():
            for c in self.copies("at_top"):
                c.wait_recv()
            for q in range(self.groups):
                for f in range(2):
                    x[q, 1 + f, pl.ds(0, w), pl.ds(EDGE, cols), :] = self.ru[q, f]
                for f in range(3):
                    x[q, f, pl.ds(0, w), pl.ds(0, EDGE), :] = blank
                    x[q, f, pl.ds(0, w), pl.ds(EDGE + cols, EDGE), :] = blank
                for k in range(w):
                    for i in range(tiles):
                        x[q, 0, w - 1 - k, pl.ds(EDGE + i * rows, rows), :] = self.pc[i, q, k]

        @pl.when(t == tiles - 1)
        def _():
            for c in self.copies("at_bottom"):
                c.wait_recv()
            for q in range(self.groups):
                for f in range(2):
                    x[q, f, pl.ds(w + rows, w), pl.ds(EDGE, cols), :] = self.rd[q, 1 + f]
                for f in range(3):
                    x[q, f, pl.ds(w + rows, w), pl.ds(0, EDGE), :] = blank
                    x[q, f, pl.ds(w + rows, w), pl.ds(EDGE + cols, EDGE), :] = blank
                for k in range(w):
                    for i in range(tiles):
                        x[q, 2, w + rows + k, pl.ds(EDGE + i * rows, rows), :] = self.pd[i, q, k]

    def drain(self):
        t = lax.axis_index("tile")
        for c in self.copies("common", "to_top", "to_bottom"):
            c.wait_send()

        @pl.when(t == 0)
        def _():
            for c in self.copies("from_top"):
                c.wait_send()

        @pl.when(t == self.tiles - 1)
        def _():
            for c in self.copies("from_bottom"):
                c.wait_send()


def blocks(rows, cols, body):
    if 3 * rows * cols <= 1024:
        body(0, 3, 0, rows)
        return
    height = max(1, min(rows, 512 // cols))
    per_face = rows // height

    @pl.loop(0, 3 * per_face)
    def _(i):
        body(i // per_face, 1, lax.rem(i, per_face) * height, height)


def conv_block(fields, weights, cols, dilation, face, faces, row, height):
    windows = []
    for tap in range(3):
        for field in fields:
            for q in range(field.shape[0]):
                got = field[q, pl.ds(face, faces), pl.ds(row, height + 2 * dilation),
                            pl.ds(EDGE + dilation * (tap - 1), cols), :]
                windows.append((tap, got.astype(BF16)))
    total = None
    for up in range(3):
        cut = [v[:, up * dilation : up * dilation + height].reshape(faces * height * cols, LANES)
               for _, v in windows]
        lhs = jnp.concatenate(cut, -1)
        rhs = jnp.concatenate([weights[up, tap] for tap in range(3)], -1)
        term = lax.dot_general(lhs, rhs, (((1,), (1,)), ((), ())), preferred_element_type=F32)
        total = term if total is None else total + term
    return total


def rounded(v):
    return v.astype(BF16).astype(F32)


def put(x, value, width, cols, face, faces, row, height):
    for q in range(x.shape[0]):
        part = value[:, q * LANES : (q + 1) * LANES].reshape(faces, height, cols, LANES)
        x[q, pl.ds(face, faces), pl.ds(width + row, height), pl.ds(EDGE, cols), :] = part


def get(x, width, cols, face, faces, row, height):
    parts = [
        x[q, pl.ds(face, faces), pl.ds(width + row, height), pl.ds(EDGE, cols), :].reshape(
            faces * height * cols, LANES)
        for q in range(x.shape[0])
    ]
    return jnp.concatenate(parts, -1) if len(parts) > 1 else parts[0]


def greet(tiles):
    t, g = lax.axis_index("tile"), lax.axis_index("face")
    faces = lax.axis_size("face")
    barrier = pltpu.get_barrier_semaphore()

    def signal(tile, face):
        pl.semaphore_signal(barrier, inc=1, device_id={"tile": tile, "face": face},
                            device_id_type=pl.DeviceIdType.MESH)

    for i in range(tiles):
        signal(i, lax.rem(g + 1, faces))
        signal(i, lax.rem(g + faces - 1, faces))
    signal(lax.rem(t + 1, tiles), g)
    signal(lax.rem(t + tiles - 1, tiles), g)
    pl.semaphore_wait(barrier, 2 * tiles + 2)


def kernel(plans, tiles, src, w_in, w_block, w_mix, w_down, w_coarse, w_decode, w_out, out, *scratch):
    halos = []
    for i, plan in enumerate(plans):
        halos.append(Halo(scratch[17 * i : 17 * i + 17], *plan, tiles))
    wide = scratch[17 * len(plans)]
    source, encoded, skip, pooled, one, two = halos
    rows, cols = source.rows, source.cols
    c_rows, c_cols = pooled.rows, pooled.cols

    def first(*at):
        face, faces, row, height = at
        v = src[pl.ds(face, faces), pl.ds(row, height), :, :]
        source.x[0, pl.ds(face, faces), pl.ds(1 + row, height), pl.ds(EDGE, cols), :] = rounded(v)

    blocks(rows, cols, first)
    greet(tiles)
    source.start()
    source.finish()

    def encode(*at):
        v = rounded(jax.nn.gelu(conv_block([source.x], w_in, cols, 1, *at)))
        put(encoded.x, v, 1, cols, *at)

    blocks(rows, cols, encode)
    encoded.start()
    encoded.finish()

    def block(*at):
        v = jax.nn.gelu(conv_block([encoded.x], w_block, cols, 1, *at)).astype(BF16)
        mixed = lax.dot_general(v, w_mix[...], (((1,), (1,)), ((), ())), preferred_element_type=F32)
        put(skip.x, rounded(get(encoded.x, 1, cols, *at) + mixed), 1, cols, *at)

    blocks(rows, cols, block)

    for f in range(3):
        for r in range(c_rows):
            total = None
            for i in range(2):
                for j in range(2):
                    v = skip.x[0, f, 1 + 2 * r + i, pl.ds(EDGE + j, c_cols, stride=2), :]
                    total = v if total is None else total + v
            pooled.x[0, f, 2 + r, pl.ds(EDGE, c_cols), :] = rounded(total * 0.25)
    pooled.start()
    skip.start()
    pooled.finish()

    def down(*at):
        v = rounded(jax.nn.gelu(conv_block([pooled.x], w_down, c_cols, 2, *at)))
        put(one.x, v, 1, c_cols, *at)

    blocks(c_rows, c_cols, down)
    one.start()
    one.finish()

    def coarse(*at):
        v = jax.nn.gelu(conv_block([one.x], w_coarse, c_cols, 1, *at))
        put(two.x, rounded(get(one.x, 1, c_cols, *at) + v), 1, c_cols, *at)

    blocks(c_rows, c_cols, coarse)
    two.start()
    skip.finish()
    two.finish()

    for q in range(wide.shape[0]):
        for f in range(3):
            for r in range(c_rows + 2):
                targets = [p for p in (2 * r - 1, 2 * r) if 0 <= p < rows + 2]
                v = two.x[q, f, r, pl.ds(EDGE, c_cols), :]
                rim_left = two.x[q, f, r, pl.ds(EDGE - 1, 1), :]
                rim_right = two.x[q, f, r, pl.ds(EDGE + c_cols, 1), :]
                for p in targets:
                    wide[q, f, p, pl.ds(EDGE, c_cols, stride=2), :] = v
                    wide[q, f, p, pl.ds(EDGE + 1, c_cols, stride=2), :] = v
                    wide[q, f, p, pl.ds(EDGE - 1, 1), :] = rim_left
                    wide[q, f, p, pl.ds(EDGE + cols, 1), :] = rim_right

    def decode(*at):
        face, faces, row, height = at
        v = jax.nn.gelu(conv_block([wide, skip.x], w_decode, cols, 1, *at)).astype(BF16)
        read = lax.dot_general(w_out[...], v, (((1,), (1,)), ((), ())), preferred_element_type=F32)
        if faces == 3:
            for f in range(3):
                out[f] = read[:, f * rows * cols : (f + 1) * rows * cols]
        else:
            size = height * cols
            out[face, :, pl.ds(pl.multiple_of(row * cols, size), size)] = read

    blocks(rows, cols, decode)
    for halo in halos:
        halo.drain()


def widened(weight, parts):
    outs = weight.shape[-2]
    sections, at = [], 0
    for size in parts:
        section = weight[..., at : at + size]
        pad = [(0, 0)] * (weight.ndim - 2)
        pad += [(0, groups_of(outs) * LANES - outs), (0, groups_of(size) * LANES - size)]
        sections.append(jnp.pad(section, pad))
        at += size
    return jnp.concatenate(sections, -1) if len(sections) > 1 else sections[0]


def shards(atmosphere, weight_in, weight_block, weight_mix, weight_down, weight_coarse,
           weight_decode, readout_matrix):
    state = atmosphere[:, 0]
    _, fields, rows, cols = state.shape
    tiles = lax.axis_size("tile")
    c0, c1 = weight_block.shape[2], weight_down.shape[2]
    src = jnp.pad(jnp.transpose(state, (0, 2, 3, 1)), [(0, 0)] * 3 + [(0, LANES - fields)])
    g0, g1 = groups_of(c0), groups_of(c1)
    plans = [
        (rows, cols, 1, 1),
        (rows, cols, 1, g0),
        (rows, cols, 1, g0),
        (rows // 2, cols // 2, 2, g0),
        (rows // 2, cols // 2, 1, g1),
        (rows // 2, cols // 2, 1, g1),
    ]
    scratch = [s for plan in plans for s in Halo.shapes(*plan, tiles)]
    scratch.append(pltpu.VMEM((g1, 3, rows + 2, cols + 2 * EDGE, LANES), F32))
    weights = [
        widened(weight_in, (fields,)),
        widened(weight_block, (c0,)),
        widened(weight_mix, (c0,)),
        widened(weight_down, (c0,)),
        widened(weight_coarse, (c1,)),
        widened(weight_decode, (c1, c0)),
        jnp.pad(readout_matrix, [(0, 0), (0, g0 * LANES - c0)]),
    ]
    read = pl.pallas_call(
        functools.partial(kernel, plans, tiles),
        out_shape=jax.ShapeDtypeStruct((3, fields, rows * cols), F32),
        in_specs=[pl.BlockSpec(memory_space=pltpu.VMEM)] * 8,
        out_specs=pl.BlockSpec(memory_space=pltpu.VMEM),
        scratch_shapes=scratch,
        compiler_params=pltpu.CompilerParams(
            collective_id=0, has_side_effects=True, vmem_limit_bytes=60 * 1024 * 1024),
    )(src, *weights)
    return (state + read.reshape(state.shape))[:, None]


def solution(mesh):
    in_specs = (P("member", "face", None, "tile", None), P(), P(), P(), P(), P(), P(), P())
    out_specs = P("member", "face", None, "tile", None)
    return jax.shard_map(shards, mesh=mesh, in_specs=in_specs, out_specs=out_specs, check_vma=False)
```

```python
import functools

import jax
import jax.numpy as jnp
from jax import lax
from jax.experimental import pallas as pl
from jax.experimental.pallas import tpu as pltpu
from jax.sharding import PartitionSpec as P

LANES = 128
EDGE = 8
TILE = 16
FIELDS = 20
F32 = jnp.float32
BF16 = jnp.bfloat16


def groups_of(channels):
    return -(-channels // LANES)


class Halo:
    def __init__(self, refs, rows, cols, width, groups, tiles):
        self.rows, self.cols, self.width = rows, cols, width
        self.groups, self.tiles = groups, tiles
        (self.x, self.stage, self.sa, self.sb, self.sc, self.sd, self.se, self.sf, self.su, self.sv,
         self.ra, self.rb, self.ru, self.rd, self.pc, self.pd, self.pe, self.pf,
         self.send, self.recv) = refs

    @staticmethod
    def sizes(rows, width, groups):
        counts = (2 * groups * width * rows, groups * width * rows, groups * width * (rows + 2 * width))
        return [-(-n // TILE) * TILE for n in counts]

    @staticmethod
    def shapes(rows, cols, width, groups, tiles):
        pair, single, long = Halo.sizes(rows, width, groups)
        strip = (groups, 3, width, cols, LANES)
        count = 10 + 2 * tiles
        shapes = [(pair,), (pair,), (single,), (single,), (tiles, long), (tiles, long), strip, strip,
                  (3, pair), (3, pair), strip, strip, (tiles, single), (tiles, single), (long,), (long,)]
        shapes = [s if s is strip else s + (LANES,) for s in shapes]
        return [
            pltpu.VMEM((groups, 3, rows + 2 * width, cols + 2 * EDGE, LANES), F32),
            pltpu.VMEM((max(pair, long), LANES), F32),
        ] + [pltpu.VMEM(s, BF16) for s in shapes] + [
            pltpu.SemaphoreType.DMA((count,)),
            pltpu.SemaphoreType.DMA((count,)),
        ]

    def pack(self, target, pieces):
        at = 0
        for piece in pieces:
            self.stage[pl.ds(at, piece.shape[0]), :] = piece
            at += piece.shape[0]
        target[...] = self.stage[pl.ds(0, target.shape[0]), :].astype(BF16)

    def unpack(self, packet):
        self.stage[pl.ds(0, packet.shape[0]), :] = packet[...].astype(F32)

    def copy(self, src, dst, send, recv, tile, face):
        return pltpu.make_async_remote_copy(
            src_ref=src, dst_ref=dst, send_sem=self.send.at[send], recv_sem=self.recv.at[recv],
            device_id={"tile": tile, "face": face}, device_id_type=pl.DeviceIdType.MESH)

    def copies(self, *names):
        tiles = self.tiles
        t, g = lax.axis_index("tile"), lax.axis_index("face")
        faces = lax.axis_size("face")
        west, east = lax.rem(g + faces - 1, faces), lax.rem(g + 1, faces)
        found = []
        for name in names:
            if name == "common":
                for step in range(3):
                    to = lax.rem(t + tiles + step - 1, tiles)
                    found.append(self.copy(self.sa, self.ra.at[step], step, step, to, west))
                    found.append(self.copy(self.sb, self.rb.at[step], 3 + step, 3 + step, to, east))
            elif name == "rows":
                up, down = lax.rem(t + tiles - 1, tiles), lax.rem(t + 1, tiles)
                found.append(self.copy(self.su, self.rd, 6, 6, up, g))
                found.append(self.copy(self.sv, self.ru, 7, 7, down, g))
            elif name == "to_top":
                found.append(self.copy(self.sc, self.pc.at[t], 8, 10 + t, 0, west))
            elif name == "to_bottom":
                found.append(self.copy(self.sd, self.pd.at[t], 9, 10 + tiles + t, tiles - 1, west))
            for i in range(tiles):
                if name == "from_top":
                    found.append(self.copy(self.se.at[i], self.pe, 10 + i, 8, i, east))
                elif name == "from_bottom":
                    found.append(self.copy(self.sf.at[i], self.pf, 10 + tiles + i, 9, i, east))
                elif name == "at_top":
                    found.append(self.copy(self.sc, self.pc.at[i], 8, 10 + i, 0, west))
                elif name == "at_bottom":
                    found.append(self.copy(self.sd, self.pd.at[i], 9, 10 + tiles + i, 0, west))
        return found

    def start(self):
        tiles, w, rows, cols, x = self.tiles, self.width, self.rows, self.cols, self.x
        t = lax.axis_index("tile")
        own = pl.ds(w, rows)
        planes = [(q, k) for q in range(self.groups) for k in range(w)]
        inner = pl.ds(EDGE, cols)
        for q in range(self.groups):
            for f in range(3):
                self.su[q, f] = x[q, f, pl.ds(w, w), inner, :].astype(BF16)
                self.sv[q, f] = x[q, f, pl.ds(rows, w), inner, :].astype(BF16)
        for c in self.copies("rows"):
            c.start()
        first = [[x[q, f, own, EDGE + k, :] for q, k in planes] for f in range(3)]
        last = [[x[q, f, own, EDGE + cols - 1 - k, :] for q, k in planes] for f in range(3)]
        self.pack(self.sc, first[0])
        self.pack(self.sd, last[2])
        for c in self.copies("to_top", "to_bottom"):
            c.start()
        self.pack(self.sa, first[1] + first[2])
        self.pack(self.sb, last[0] + last[1])
        for c in self.copies("common"):
            c.start()

        def long(i, face, row_of):
            cells = pl.ds(EDGE + i * rows - w, rows + 2 * w)
            return [x[q, face, row_of(k), cells, :] for q, k in planes]

        @pl.when(t == 0)
        def _():
            for i, c in enumerate(self.copies("from_top")):
                self.pack(self.se.at[i], long(i, 0, lambda k: w + k))
                c.start()

        @pl.when(t == tiles - 1)
        def _():
            for i, c in enumerate(self.copies("from_bottom")):
                self.pack(self.sf.at[i], long(i, 2, lambda k: w + rows - 1 - k))
                c.start()

    def finish(self):
        tiles, w, rows, cols, x = self.tiles, self.width, self.rows, self.cols, self.x
        t = lax.axis_index("tile")
        for c in self.copies("common", "rows"):
            c.wait_recv()
        self.copy(self.se.at[0], self.pe, 10, 8, 0, 0).wait_recv()
        self.copy(self.sf.at[0], self.pf, 10, 9, 0, 0).wait_recv()
        planes = [(q, k) for q in range(self.groups) for k in range(w)]
        stage = self.stage
        for got, base, sign in ((self.rb, 1, -1), (self.ra, 0, 1)):
            for step in range(3):
                self.unpack(got.at[step])
                for f in range(2):
                    for n, (q, k) in enumerate(planes):
                        col = EDGE - 1 - k if sign < 0 else EDGE + cols + k
                        at = (f * len(planes) + n) * rows
                        if step == 0:
                            x[q, base + f, pl.ds(w + rows, w), col, :] = stage[pl.ds(at, w), :]
                        elif step == 1:
                            x[q, base + f, pl.ds(w, rows), col, :] = stage[pl.ds(at, rows), :]
                        else:
                            x[q, base + f, pl.ds(0, w), col, :] = stage[pl.ds(at + rows - w, w), :]
        for got, face, sign in ((self.pe, 0, -1), (self.pf, 2, 1)):
            self.unpack(got)
            for n, (q, k) in enumerate(planes):
                col = EDGE - 1 - k if sign < 0 else EDGE + cols + k
                x[q, face, :, col, :] = stage[pl.ds(n * (rows + 2 * w), rows + 2 * w), :]
        inner = pl.ds(EDGE, cols)
        for q in range(self.groups):
            for f in range(3):
                x[q, f, pl.ds(0, w), inner, :] = self.ru[q, f].astype(F32)
                x[q, f, pl.ds(w + rows, w), inner, :] = self.rd[q, f].astype(F32)
        blank = jnp.zeros((w, EDGE, LANES), F32)

        def no_corners(q, at):
            for f in range(3):
                x[q, f, pl.ds(at, w), pl.ds(0, EDGE), :] = blank
                x[q, f, pl.ds(at, w), pl.ds(EDGE + cols, EDGE), :] = blank

        def polar(name, packets, face, row_of):
            for i, c in enumerate(self.copies(name)):
                c.wait_recv()
                self.unpack(packets.at[i])
                for n, (q, k) in enumerate(planes):
                    x[q, face, row_of(k), pl.ds(EDGE + i * rows, rows), :] = stage[pl.ds(n * rows, rows), :]

        @pl.when(t == 0)
        def _():
            for q in range(self.groups):
                for f in range(2):
                    x[q, 1 + f, pl.ds(0, w), inner, :] = self.ru[q, f].astype(F32)
                no_corners(q, 0)
            polar("at_top", self.pc, 0, lambda k: w - 1 - k)

        @pl.when(t == tiles - 1)
        def _():
            for q in range(self.groups):
                for f in range(2):
                    x[q, f, pl.ds(w + rows, w), inner, :] = self.rd[q, 1 + f].astype(F32)
                no_corners(q, w + rows)
            polar("at_bottom", self.pd, 2, lambda k: w + rows + k)

    def drain(self):
        t = lax.axis_index("tile")
        for c in self.copies("common", "rows", "to_top", "to_bottom"):
            c.wait_send()

        @pl.when(t == 0)
        def _():
            for c in self.copies("from_top"):
                c.wait_send()

        @pl.when(t == self.tiles - 1)
        def _():
            for c in self.copies("from_bottom"):
                c.wait_send()


def blocks(rows, cols, body):
    if 3 * rows * cols <= 1024:
        body(0, 3, 0, rows)
        return
    height = max(1, min(rows, 512 // cols))
    per_face = rows // height

    @pl.loop(0, 3 * per_face)
    def _(i):
        body(i // per_face, 1, lax.rem(i, per_face) * height, height)


def conv_block(fields, weights, cols, dilation, face, faces, row, height):
    windows = []
    for tap in range(3):
        for field in fields:
            for q in range(field.shape[0]):
                got = field[q, pl.ds(face, faces), pl.ds(row, height + 2 * dilation),
                            pl.ds(EDGE + dilation * (tap - 1), cols), :]
                windows.append((tap, got.astype(BF16)))
    total = None
    for up in range(3):
        cut = [v[:, up * dilation : up * dilation + height].reshape(faces * height * cols, LANES)
               for _, v in windows]
        lhs = jnp.concatenate(cut, -1)
        term = lax.dot_general(lhs, weights[up], (((1,), (1,)), ((), ())), preferred_element_type=F32)
        total = term if total is None else total + term
    return total


def rounded(v):
    return v.astype(BF16).astype(F32)


def put(x, value, width, cols, face, faces, row, height):
    for q in range(x.shape[0]):
        part = value[:, q * LANES : (q + 1) * LANES].reshape(faces, height, cols, LANES)
        x[q, pl.ds(face, faces), pl.ds(width + row, height), pl.ds(EDGE, cols), :] = part


def get(x, width, cols, face, faces, row, height):
    parts = [
        x[q, pl.ds(face, faces), pl.ds(width + row, height), pl.ds(EDGE, cols), :].reshape(
            faces * height * cols, LANES)
        for q in range(x.shape[0])
    ]
    return jnp.concatenate(parts, -1) if len(parts) > 1 else parts[0]


def greet_first(tiles):
    t, g = lax.axis_index("tile"), lax.axis_index("face")
    faces = lax.axis_size("face")
    barrier = pltpu.get_barrier_semaphore()

    def signal(tile, face):
        pl.semaphore_signal(barrier, inc=1, device_id={"tile": tile, "face": face},
                            device_id_type=pl.DeviceIdType.MESH)

    for i in range(tiles):
        signal(i, lax.rem(g + 1, faces))
        signal(i, lax.rem(g + faces - 1, faces))
    signal(lax.rem(t + 1, tiles), g)
    signal(lax.rem(t + tiles - 1, tiles), g)


def greet_wait(tiles):
    pl.semaphore_wait(pltpu.get_barrier_semaphore(), 2 * tiles + 2)


def widen(wide, weight, parts):
    outs = weight.shape[2]
    step = sum(groups_of(size) for size in parts) * LANES
    wide[...] = jnp.zeros_like(wide)
    for up in range(3):
        for tap in range(3):
            at, begin = tap * step, 0
            for size in parts:
                wide[up, pl.ds(0, outs), pl.ds(at, size)] = weight[up, tap, :, begin : begin + size]
                at += groups_of(size) * LANES
                begin += size


def kernel(plans, tiles, src, w_in, w_block, w_mix, w_down, w_coarse, w_decode, w_out, out, *scratch):
    halos = []
    for i, plan in enumerate(plans):
        halos.append(Halo(scratch[FIELDS * i : FIELDS * i + FIELDS], *plan, tiles))
    wide, k_in, k_block, k_mix, k_down, k_coarse, k_decode, k_out = scratch[FIELDS * len(plans) :]
    source, encoded, skip, pooled, one, two = halos
    rows, cols = source.rows, source.cols
    c_rows, c_cols = pooled.rows, pooled.cols

    greet_first(tiles)

    def first(*at):
        face, faces, row, height = at
        v = rounded(src[pl.ds(face, faces), pl.ds(row, height), :, :])
        place = (0, pl.ds(face, faces), pl.ds(1 + row, height), pl.ds(EDGE, cols))
        source.x[place] = jnp.zeros((faces, height, cols, LANES), F32)
        source.x[place + (pl.ds(0, src.shape[3]),)] = v

    blocks(rows, cols, first)
    greet_wait(tiles)
    source.start()
    fields, c0, c1 = w_in.shape[3], w_block.shape[3], w_coarse.shape[3]
    widen(k_in, w_in, (fields,))
    widen(k_block, w_block, (c0,))
    k_mix[...] = jnp.zeros_like(k_mix)
    k_mix[pl.ds(0, c0), pl.ds(0, c0)] = w_mix[...]
    k_out[...] = jnp.zeros_like(k_out)
    k_out[:, pl.ds(0, c0)] = w_out[...]
    source.finish()

    def encode(*at):
        v = rounded(jax.nn.gelu(conv_block([source.x], k_in, cols, 1, *at)))
        put(encoded.x, v, 1, cols, *at)

    blocks(rows, cols, encode)
    encoded.start()
    widen(k_down, w_down, (c0,))
    widen(k_coarse, w_coarse, (c1,))
    widen(k_decode, w_decode, (c1, c0))
    encoded.finish()

    def block(*at):
        v = jax.nn.gelu(conv_block([encoded.x], k_block, cols, 1, *at)).astype(BF16)
        mixed = lax.dot_general(v, k_mix[...], (((1,), (1,)), ((), ())), preferred_element_type=F32)
        put(skip.x, rounded(get(encoded.x, 1, cols, *at) + mixed), 1, cols, *at)

    blocks(rows, cols, block)

    for f in range(3):
        for r in range(c_rows):
            total = None
            for i in range(2):
                for j in range(2):
                    v = skip.x[0, f, 1 + 2 * r + i, pl.ds(EDGE + j, c_cols, stride=2), :]
                    total = v if total is None else total + v
            pooled.x[0, f, 2 + r, pl.ds(EDGE, c_cols), :] = rounded(total * 0.25)
    pooled.start()
    skip.start()
    pooled.finish()

    def down(*at):
        v = rounded(jax.nn.gelu(conv_block([pooled.x], k_down, c_cols, 2, *at)))
        put(one.x, v, 1, c_cols, *at)

    blocks(c_rows, c_cols, down)
    one.start()
    one.finish()

    def coarse(*at):
        v = jax.nn.gelu(conv_block([one.x], k_coarse, c_cols, 1, *at))
        put(two.x, rounded(get(one.x, 1, c_cols, *at) + v), 1, c_cols, *at)

    blocks(c_rows, c_cols, coarse)
    two.start()
    skip.finish()
    two.finish()

    for q in range(wide.shape[0]):
        for f in range(3):
            for r in range(c_rows + 2):
                targets = [p for p in (2 * r - 1, 2 * r) if 0 <= p < rows + 2]
                v = two.x[q, f, r, pl.ds(EDGE, c_cols), :]
                rim_left = two.x[q, f, r, pl.ds(EDGE - 1, 1), :]
                rim_right = two.x[q, f, r, pl.ds(EDGE + c_cols, 1), :]
                for p in targets:
                    wide[q, f, p, pl.ds(EDGE, c_cols, stride=2), :] = v
                    wide[q, f, p, pl.ds(EDGE + 1, c_cols, stride=2), :] = v
                    wide[q, f, p, pl.ds(EDGE - 1, 1), :] = rim_left
                    wide[q, f, p, pl.ds(EDGE + cols, 1), :] = rim_right

    def decode(*at):
        face, faces, row, height = at
        v = jax.nn.gelu(conv_block([wide, skip.x], k_decode, cols, 1, *at)).astype(BF16)
        read = lax.dot_general(k_out[...], v, (((1,), (1,)), ((), ())), preferred_element_type=F32)
        if faces == 3:
            for f in range(3):
                out[f] = read[:, f * rows * cols : (f + 1) * rows * cols]
        else:
            size = height * cols
            out[face, :, pl.ds(pl.multiple_of(row * cols, size), size)] = read

    blocks(rows, cols, decode)
    for halo in halos:
        halo.drain()


def shards(atmosphere, weight_in, weight_block, weight_mix, weight_down, weight_coarse,
           weight_decode, readout_matrix):
    state = atmosphere[:, 0]
    _, fields, rows, cols = state.shape
    tiles = lax.axis_size("tile")
    c0, c1 = weight_block.shape[2], weight_down.shape[2]
    src = jnp.transpose(state, (0, 2, 3, 1))
    g0, g1 = groups_of(c0), groups_of(c1)
    plans = [
        (rows, cols, 1, 1),
        (rows, cols, 1, g0),
        (rows, cols, 1, g0),
        (rows // 2, cols // 2, 2, g0),
        (rows // 2, cols // 2, 1, g1),
        (rows // 2, cols // 2, 1, g1),
    ]
    scratch = [s for plan in plans for s in Halo.shapes(*plan, tiles)]
    scratch.append(pltpu.VMEM((g1, 3, rows + 2, cols + 2 * EDGE, LANES), F32))
    scratch += [
        pltpu.VMEM(s, BF16)
        for s in (
            (3, g0 * LANES, 3 * LANES),
            (3, g0 * LANES, 3 * g0 * LANES),
            (g0 * LANES, g0 * LANES),
            (3, g1 * LANES, 3 * g0 * LANES),
            (3, g1 * LANES, 3 * g1 * LANES),
            (3, g0 * LANES, 3 * (g1 + g0) * LANES),
            (fields, g0 * LANES),
        )
    ]
    weights = [weight_in, weight_block, weight_mix, weight_down, weight_coarse, weight_decode,
               readout_matrix]
    read = pl.pallas_call(
        functools.partial(kernel, plans, tiles),
        out_shape=jax.ShapeDtypeStruct((3, fields, rows * cols), F32),
        in_specs=[pl.BlockSpec(memory_space=pltpu.VMEM)] * 8,
        out_specs=pl.BlockSpec(memory_space=pltpu.VMEM),
        scratch_shapes=scratch,
        compiler_params=pltpu.CompilerParams(
            collective_id=0, has_side_effects=True, vmem_limit_bytes=60 * 1024 * 1024),
    )(src, *weights)
    return (state + read.reshape(state.shape))[:, None]


def solution(mesh):
    in_specs = (P("member", "face", None, "tile", None), P(), P(), P(), P(), P(), P(), P())
    out_specs = P("member", "face", None, "tile", None)
    return jax.shard_map(shards, mesh=mesh, in_specs=in_specs, out_specs=out_specs, check_vma=False)
```

```python
import functools

import jax
import jax.numpy as jnp
from jax import lax
from jax.experimental import pallas as pl
from jax.experimental.pallas import tpu as pltpu
from jax.sharding import PartitionSpec as P

LANES = 128
EDGE = 8
TILE = 16
FIELDS = 20
F32 = jnp.float32
BF16 = jnp.bfloat16


def groups_of(channels):
    return -(-channels // LANES)


class Halo:
    def __init__(self, refs, rows, cols, width, groups, tiles):
        self.rows, self.cols, self.width = rows, cols, width
        self.groups, self.tiles = groups, tiles
        (self.x, self.stage, self.sa, self.sb, self.sc, self.sd, self.se, self.sf, self.su, self.sv,
         self.ra, self.rb, self.ru, self.rd, self.pc, self.pd, self.pe, self.pf,
         self.send, self.recv) = refs

    @staticmethod
    def sizes(rows, width, groups):
        counts = (2 * groups * width * rows, groups * width * rows, groups * width * (rows + 2 * width))
        return [-(-n // TILE) * TILE for n in counts]

    @staticmethod
    def shapes(rows, cols, width, groups, tiles):
        pair, single, long = Halo.sizes(rows, width, groups)
        strip = (groups, 3, width, cols, LANES)
        count = 10 + 2 * tiles
        shapes = [(pair,), (pair,), (single,), (single,), (tiles, long), (tiles, long), strip, strip,
                  (3, pair), (3, pair), strip, strip, (tiles, single), (tiles, single), (long,), (long,)]
        shapes = [s if s is strip else s + (LANES,) for s in shapes]
        return [
            pltpu.VMEM((groups, 3, rows + 2 * width, cols + 2 * EDGE, LANES), F32),
            pltpu.VMEM((max(pair, long), LANES), F32),
        ] + [pltpu.VMEM(s, BF16) for s in shapes] + [
            pltpu.SemaphoreType.DMA((count,)),
            pltpu.SemaphoreType.DMA((count,)),
        ]

    def pack(self, target, pieces):
        at = 0
        for piece in pieces:
            self.stage[pl.ds(at, piece.shape[0]), :] = piece
            at += piece.shape[0]
        target[...] = self.stage[pl.ds(0, target.shape[0]), :].astype(BF16)

    def unpack(self, packet):
        self.stage[pl.ds(0, packet.shape[0]), :] = packet[...].astype(F32)

    def copy(self, src, dst, send, recv, tile, face):
        return pltpu.make_async_remote_copy(
            src_ref=src, dst_ref=dst, send_sem=self.send.at[send], recv_sem=self.recv.at[recv],
            device_id={"tile": tile, "face": face}, device_id_type=pl.DeviceIdType.MESH)

    def copies(self, *names):
        tiles = self.tiles
        t, g = lax.axis_index("tile"), lax.axis_index("face")
        faces = lax.axis_size("face")
        west, east = lax.rem(g + faces - 1, faces), lax.rem(g + 1, faces)
        found = []
        for name in names:
            if name == "common":
                for step in range(3):
                    to = lax.rem(t + tiles + step - 1, tiles)
                    found.append(self.copy(self.sa, self.ra.at[step], step, step, to, west))
                    found.append(self.copy(self.sb, self.rb.at[step], 3 + step, 3 + step, to, east))
            elif name == "rows":
                up, down = lax.rem(t + tiles - 1, tiles), lax.rem(t + 1, tiles)
                found.append(self.copy(self.su, self.rd, 6, 6, up, g))
                found.append(self.copy(self.sv, self.ru, 7, 7, down, g))
            elif name == "to_top":
                found.append(self.copy(self.sc, self.pc.at[t], 8, 10 + t, 0, west))
            elif name == "to_bottom":
                found.append(self.copy(self.sd, self.pd.at[t], 9, 10 + tiles + t, tiles - 1, west))
            for i in range(tiles):
                if name == "from_top":
                    found.append(self.copy(self.se.at[i], self.pe, 10 + i, 8, i, east))
                elif name == "from_bottom":
                    found.append(self.copy(self.sf.at[i], self.pf, 10 + tiles + i, 9, i, east))
                elif name == "at_top":
                    found.append(self.copy(self.sc, self.pc.at[i], 8, 10 + i, 0, west))
                elif name == "at_bottom":
                    found.append(self.copy(self.sd, self.pd.at[i], 9, 10 + tiles + i, 0, west))
        return found

    def start(self):
        tiles, w, rows, cols, x = self.tiles, self.width, self.rows, self.cols, self.x
        t = lax.axis_index("tile")
        own = pl.ds(w, rows)
        planes = [(q, k) for q in range(self.groups) for k in range(w)]
        inner = pl.ds(EDGE, cols)
        for q in range(self.groups):
            for f in range(3):
                self.su[q, f] = x[q, f, pl.ds(w, w), inner, :].astype(BF16)
                self.sv[q, f] = x[q, f, pl.ds(rows, w), inner, :].astype(BF16)
        for c in self.copies("rows"):
            c.start()
        first = [[x[q, f, own, EDGE + k, :] for q, k in planes] for f in range(3)]
        last = [[x[q, f, own, EDGE + cols - 1 - k, :] for q, k in planes] for f in range(3)]
        self.pack(self.sc, first[0])
        self.pack(self.sd, last[2])
        for c in self.copies("to_top", "to_bottom"):
            c.start()
        self.pack(self.sa, first[1] + first[2])
        self.pack(self.sb, last[0] + last[1])
        for c in self.copies("common"):
            c.start()

        def long(i, face, row_of):
            cells = pl.ds(EDGE + i * rows - w, rows + 2 * w)
            return [x[q, face, row_of(k), cells, :] for q, k in planes]

        @pl.when(t == 0)
        def _():
            for i, c in enumerate(self.copies("from_top")):
                self.pack(self.se.at[i], long(i, 0, lambda k: w + k))
                c.start()

        @pl.when(t == tiles - 1)
        def _():
            for i, c in enumerate(self.copies("from_bottom")):
                self.pack(self.sf.at[i], long(i, 2, lambda k: w + rows - 1 - k))
                c.start()

    def finish(self):
        tiles, w, rows, cols, x = self.tiles, self.width, self.rows, self.cols, self.x
        t = lax.axis_index("tile")
        for c in self.copies("common", "rows"):
            c.wait_recv()
        self.copy(self.se.at[0], self.pe, 10, 8, 0, 0).wait_recv()
        self.copy(self.sf.at[0], self.pf, 10, 9, 0, 0).wait_recv()
        planes = [(q, k) for q in range(self.groups) for k in range(w)]
        stage = self.stage
        for got, base, sign in ((self.rb, 1, -1), (self.ra, 0, 1)):
            for step in range(3):
                self.unpack(got.at[step])
                for f in range(2):
                    for n, (q, k) in enumerate(planes):
                        col = EDGE - 1 - k if sign < 0 else EDGE + cols + k
                        at = (f * len(planes) + n) * rows
                        if step == 0:
                            x[q, base + f, pl.ds(w + rows, w), col, :] = stage[pl.ds(at, w), :]
                        elif step == 1:
                            x[q, base + f, pl.ds(w, rows), col, :] = stage[pl.ds(at, rows), :]
                        else:
                            x[q, base + f, pl.ds(0, w), col, :] = stage[pl.ds(at + rows - w, w), :]
        for got, face, sign in ((self.pe, 0, -1), (self.pf, 2, 1)):
            self.unpack(got)
            for n, (q, k) in enumerate(planes):
                col = EDGE - 1 - k if sign < 0 else EDGE + cols + k
                x[q, face, :, col, :] = stage[pl.ds(n * (rows + 2 * w), rows + 2 * w), :]
        inner = pl.ds(EDGE, cols)
        for q in range(self.groups):
            for f in range(3):
                x[q, f, pl.ds(0, w), inner, :] = self.ru[q, f].astype(F32)
                x[q, f, pl.ds(w + rows, w), inner, :] = self.rd[q, f].astype(F32)
        blank = jnp.zeros((w, EDGE, LANES), F32)

        def no_corners(q, at):
            for f in range(3):
                x[q, f, pl.ds(at, w), pl.ds(0, EDGE), :] = blank
                x[q, f, pl.ds(at, w), pl.ds(EDGE + cols, EDGE), :] = blank

        def polar(name, packets, face, row_of):
            for i, c in enumerate(self.copies(name)):
                c.wait_recv()
                self.unpack(packets.at[i])
                for n, (q, k) in enumerate(planes):
                    x[q, face, row_of(k), pl.ds(EDGE + i * rows, rows), :] = stage[pl.ds(n * rows, rows), :]

        @pl.when(t == 0)
        def _():
            for q in range(self.groups):
                for f in range(2):
                    x[q, 1 + f, pl.ds(0, w), inner, :] = self.ru[q, f].astype(F32)
                no_corners(q, 0)
            polar("at_top", self.pc, 0, lambda k: w - 1 - k)

        @pl.when(t == tiles - 1)
        def _():
            for q in range(self.groups):
                for f in range(2):
                    x[q, f, pl.ds(w + rows, w), inner, :] = self.rd[q, 1 + f].astype(F32)
                no_corners(q, w + rows)
            polar("at_bottom", self.pd, 2, lambda k: w + rows + k)

    def drain(self):
        t = lax.axis_index("tile")
        for c in self.copies("common", "rows", "to_top", "to_bottom"):
            c.wait_send()

        @pl.when(t == 0)
        def _():
            for c in self.copies("from_top"):
                c.wait_send()

        @pl.when(t == self.tiles - 1)
        def _():
            for c in self.copies("from_bottom"):
                c.wait_send()


def blocks(rows, cols, body):
    if 3 * rows * cols <= 1024:
        body(0, 3, 0, rows)
        return
    height = max(1, min(rows, 512 // cols))
    per_face = rows // height

    @pl.loop(0, 3 * per_face)
    def _(i):
        body(i // per_face, 1, lax.rem(i, per_face) * height, height)


def conv_block(fields, weights, cols, dilation, face, faces, row, height):
    windows = []
    for tap in range(3):
        for field in fields:
            for q in range(field.shape[0]):
                got = field[q, pl.ds(face, faces), pl.ds(row, height + 2 * dilation),
                            pl.ds(EDGE + dilation * (tap - 1), cols), :]
                windows.append((tap, got.astype(BF16)))
    total = None
    for up in range(3):
        cut = [v[:, up * dilation : up * dilation + height].reshape(faces * height * cols, LANES)
               for _, v in windows]
        lhs = jnp.concatenate(cut, -1)
        rhs = weights[up]
        across = 0 if rhs.shape[0] == lhs.shape[1] else 1
        term = lax.dot_general(lhs, rhs, (((1,), (across,)), ((), ())), preferred_element_type=F32)
        total = term if total is None else total + term
    return total


def rounded(v):
    return v.astype(BF16).astype(F32)


def put(x, value, width, cols, face, faces, row, height):
    for q in range(x.shape[0]):
        part = value[:, q * LANES : (q + 1) * LANES].reshape(faces, height, cols, LANES)
        x[q, pl.ds(face, faces), pl.ds(width + row, height), pl.ds(EDGE, cols), :] = part


def get(x, width, cols, face, faces, row, height):
    parts = [
        x[q, pl.ds(face, faces), pl.ds(width + row, height), pl.ds(EDGE, cols), :].reshape(
            faces * height * cols, LANES)
        for q in range(x.shape[0])
    ]
    return jnp.concatenate(parts, -1) if len(parts) > 1 else parts[0]


def greet_first(tiles):
    t, g = lax.axis_index("tile"), lax.axis_index("face")
    faces = lax.axis_size("face")
    barrier = pltpu.get_barrier_semaphore()

    def signal(tile, face):
        pl.semaphore_signal(barrier, inc=1, device_id={"tile": tile, "face": face},
                            device_id_type=pl.DeviceIdType.MESH)

    for i in range(tiles):
        signal(i, lax.rem(g + 1, faces))
        signal(i, lax.rem(g + faces - 1, faces))
    signal(lax.rem(t + 1, tiles), g)
    signal(lax.rem(t + tiles - 1, tiles), g)


def greet_wait(tiles):
    pl.semaphore_wait(pltpu.get_barrier_semaphore(), 2 * tiles + 2)


def heighten(tall, weight, parts):
    outs = weight.shape[3]
    step = sum(groups_of(size) for size in parts) * LANES
    tall[...] = jnp.zeros_like(tall)
    for up in range(3):
        for tap in range(3):
            at, begin = tap * step, 0
            for size in parts:
                tall[up, pl.ds(at, size), pl.ds(0, outs)] = weight[up, tap, begin : begin + size, :]
                at += groups_of(size) * LANES
                begin += size


def widen(wide, weight, parts):
    outs = weight.shape[2]
    step = sum(groups_of(size) for size in parts) * LANES
    wide[...] = jnp.zeros_like(wide)
    for up in range(3):
        for tap in range(3):
            at, begin = tap * step, 0
            for size in parts:
                wide[up, pl.ds(0, outs), pl.ds(at, size)] = weight[up, tap, :, begin : begin + size]
                at += groups_of(size) * LANES
                begin += size


def kernel(plans, tiles, state, src, w_in, w_block, w_mix, w_down, w_coarse, w_decode, w_out, out, *scratch):
    halos = []
    for i, plan in enumerate(plans):
        halos.append(Halo(scratch[FIELDS * i : FIELDS * i + FIELDS], *plan, tiles))
    wide, k_in, k_block, k_mix, k_down, k_coarse, k_decode, k_out = scratch[FIELDS * len(plans) :]
    source, encoded, skip, pooled, one, two = halos
    rows, cols = source.rows, source.cols
    c_rows, c_cols = pooled.rows, pooled.cols

    greet_first(tiles)

    def first(*at):
        face, faces, row, height = at
        v = rounded(src[pl.ds(face, faces), pl.ds(row, height), :, :])
        place = (0, pl.ds(face, faces), pl.ds(1 + row, height), pl.ds(EDGE, cols))
        source.x[place] = jnp.zeros((faces, height, cols, LANES), F32)
        source.x[place + (pl.ds(0, src.shape[3]),)] = v

    blocks(rows, cols, first)
    greet_wait(tiles)
    source.start()
    fields, c0, c1 = w_in.shape[2], w_block.shape[3], w_coarse.shape[3]
    heighten(k_in, w_in, (fields,))
    widen(k_block, w_block, (c0,))
    k_mix[...] = jnp.zeros_like(k_mix)
    k_mix[pl.ds(0, c0), pl.ds(0, c0)] = w_mix[...]
    k_out[...] = jnp.zeros_like(k_out)
    k_out[:, pl.ds(0, c0)] = w_out[...]
    source.finish()

    def encode(*at):
        v = rounded(jax.nn.gelu(conv_block([source.x], k_in, cols, 1, *at)))
        put(encoded.x, v, 1, cols, *at)

    blocks(rows, cols, encode)
    encoded.start()
    widen(k_down, w_down, (c0,))
    widen(k_coarse, w_coarse, (c1,))
    heighten(k_decode, w_decode, (c1, c0))
    encoded.finish()

    def block(*at):
        v = jax.nn.gelu(conv_block([encoded.x], k_block, cols, 1, *at)).astype(BF16)
        mixed = lax.dot_general(v, k_mix[...], (((1,), (1,)), ((), ())), preferred_element_type=F32)
        put(skip.x, rounded(get(encoded.x, 1, cols, *at) + mixed), 1, cols, *at)

    blocks(rows, cols, block)

    for f in range(3):
        for r in range(c_rows):
            total = None
            for i in range(2):
                for j in range(2):
                    v = skip.x[0, f, 1 + 2 * r + i, pl.ds(EDGE + j, c_cols, stride=2), :]
                    total = v if total is None else total + v
            pooled.x[0, f, 2 + r, pl.ds(EDGE, c_cols), :] = rounded(total * 0.25)
    pooled.start()
    skip.start()
    pooled.finish()

    def down(*at):
        v = rounded(jax.nn.gelu(conv_block([pooled.x], k_down, c_cols, 2, *at)))
        put(one.x, v, 1, c_cols, *at)

    blocks(c_rows, c_cols, down)
    one.start()
    one.finish()

    def coarse(*at):
        v = jax.nn.gelu(conv_block([one.x], k_coarse, c_cols, 1, *at))
        put(two.x, rounded(get(one.x, 1, c_cols, *at) + v), 1, c_cols, *at)

    blocks(c_rows, c_cols, coarse)
    two.start()
    skip.finish()
    two.finish()

    for q in range(wide.shape[0]):
        for f in range(3):
            for r in range(c_rows + 2):
                targets = [p for p in (2 * r - 1, 2 * r) if 0 <= p < rows + 2]
                v = two.x[q, f, r, pl.ds(EDGE, c_cols), :]
                rim_left = two.x[q, f, r, pl.ds(EDGE - 1, 1), :]
                rim_right = two.x[q, f, r, pl.ds(EDGE + c_cols, 1), :]
                for p in targets:
                    wide[q, f, p, pl.ds(EDGE, c_cols, stride=2), :] = v
                    wide[q, f, p, pl.ds(EDGE + 1, c_cols, stride=2), :] = v
                    wide[q, f, p, pl.ds(EDGE - 1, 1), :] = rim_left
                    wide[q, f, p, pl.ds(EDGE + cols, 1), :] = rim_right

    def decode(*at):
        face, faces, row, height = at
        v = jax.nn.gelu(conv_block([wide, skip.x], k_decode, cols, 1, *at)).astype(BF16)
        read = lax.dot_general(k_out[...], v, (((1,), (1,)), ((), ())), preferred_element_type=F32)
        for f in range(faces):
            for r in range(height):
                at = (f * height + r) * cols
                out[face + f, :, row + r, :] = state[face + f, :, row + r, :] + read[:, at : at + cols]

    blocks(rows, cols, decode)
    for halo in halos:
        halo.drain()


def shards(atmosphere, weight_in, weight_block, weight_mix, weight_down, weight_coarse,
           weight_decode, readout_matrix):
    state = atmosphere[:, 0]
    _, fields, rows, cols = state.shape
    tiles = lax.axis_size("tile")
    c0, c1 = weight_block.shape[2], weight_down.shape[2]
    src = jnp.transpose(state, (0, 2, 3, 1))
    g0, g1 = groups_of(c0), groups_of(c1)
    plans = [
        (rows, cols, 1, 1),
        (rows, cols, 1, g0),
        (rows, cols, 1, g0),
        (rows // 2, cols // 2, 2, g0),
        (rows // 2, cols // 2, 1, g1),
        (rows // 2, cols // 2, 1, g1),
    ]
    scratch = [s for plan in plans for s in Halo.shapes(*plan, tiles)]
    scratch.append(pltpu.VMEM((g1, 3, rows + 2, cols + 2 * EDGE, LANES), F32))
    scratch += [
        pltpu.VMEM(s, BF16)
        for s in (
            (3, 3 * LANES, g0 * LANES),
            (3, g0 * LANES, 3 * g0 * LANES),
            (g0 * LANES, g0 * LANES),
            (3, g1 * LANES, 3 * g0 * LANES),
            (3, g1 * LANES, 3 * g1 * LANES),
            (3, 3 * (g1 + g0) * LANES, g0 * LANES),
            (fields, g0 * LANES),
        )
    ]
    weights = [jnp.swapaxes(weight_in, 2, 3), weight_block, weight_mix, weight_down, weight_coarse,
               jnp.swapaxes(weight_decode, 2, 3), readout_matrix]
    advanced = pl.pallas_call(
        functools.partial(kernel, plans, tiles),
        out_shape=jax.ShapeDtypeStruct((3, fields, rows, cols), F32),
        in_specs=[pl.BlockSpec(memory_space=pltpu.VMEM)] * 9,
        out_specs=pl.BlockSpec(memory_space=pltpu.VMEM),
        scratch_shapes=scratch,
        compiler_params=pltpu.CompilerParams(
            collective_id=0, has_side_effects=True, vmem_limit_bytes=60 * 1024 * 1024),
    )(state, src, *weights)
    return advanced[:, None]


def solution(mesh):
    in_specs = (P("member", "face", None, "tile", None), P(), P(), P(), P(), P(), P(), P())
    out_specs = P("member", "face", None, "tile", None)
    return jax.shard_map(shards, mesh=mesh, in_specs=in_specs, out_specs=out_specs, check_vma=False)
```

```python
import functools

import jax
import jax.numpy as jnp
from jax import lax
from jax.experimental import pallas as pl
from jax.experimental.pallas import tpu as pltpu
from jax.sharding import PartitionSpec as P

LANES = 128
EDGE = 8
TILE = 16
FIELDS = 20
F32 = jnp.float32
BF16 = jnp.bfloat16


def groups_of(channels):
    return -(-channels // LANES)


class Halo:
    def __init__(self, refs, rows, cols, width, groups, tiles):
        self.rows, self.cols, self.width = rows, cols, width
        self.groups, self.tiles = groups, tiles
        (self.x, self.stage, self.sa, self.sb, self.sc, self.sd, self.se, self.sf, self.su, self.sv,
         self.ra, self.rb, self.ru, self.rd, self.pc, self.pd, self.pe, self.pf,
         self.send, self.recv) = refs

    @staticmethod
    def sizes(rows, width, groups):
        counts = (2 * groups * width * rows, groups * width * rows, groups * width * (rows + 2 * width))
        return [-(-n // TILE) * TILE for n in counts]

    @staticmethod
    def shapes(rows, cols, width, groups, tiles):
        pair, single, long = Halo.sizes(rows, width, groups)
        strip = (groups, 3, width, cols, LANES)
        count = 10 + 2 * tiles
        shapes = [(pair,), (pair,), (single,), (single,), (tiles, long), (tiles, long), strip, strip,
                  (3, pair), (3, pair), strip, strip, (tiles, single), (tiles, single), (long,), (long,)]
        shapes = [s if s is strip else s + (LANES,) for s in shapes]
        return [
            pltpu.VMEM((groups, 3, rows + 2 * width, cols + 2 * EDGE, LANES), F32),
            pltpu.VMEM((max(pair, long), LANES), F32),
        ] + [pltpu.VMEM(s, BF16) for s in shapes] + [
            pltpu.SemaphoreType.DMA((count,)),
            pltpu.SemaphoreType.DMA((count,)),
        ]

    def pack(self, target, pieces):
        at = 0
        for piece in pieces:
            self.stage[pl.ds(at, piece.shape[0]), :] = piece
            at += piece.shape[0]
        target[...] = self.stage[pl.ds(0, target.shape[0]), :].astype(BF16)

    def unpack(self, packet):
        self.stage[pl.ds(0, packet.shape[0]), :] = packet[...].astype(F32)

    def copy(self, src, dst, send, recv, tile, face):
        return pltpu.make_async_remote_copy(
            src_ref=src, dst_ref=dst, send_sem=self.send.at[send], recv_sem=self.recv.at[recv],
            device_id={"tile": tile, "face": face}, device_id_type=pl.DeviceIdType.MESH)

    def copies(self, *names):
        tiles = self.tiles
        t, g = lax.axis_index("tile"), lax.axis_index("face")
        faces = lax.axis_size("face")
        west, east = lax.rem(g + faces - 1, faces), lax.rem(g + 1, faces)
        found = []
        for name in names:
            if name == "common":
                for step in range(3):
                    to = lax.rem(t + tiles + step - 1, tiles)
                    found.append(self.copy(self.sa, self.ra.at[step], step, step, to, west))
                    found.append(self.copy(self.sb, self.rb.at[step], 3 + step, 3 + step, to, east))
            elif name == "rows":
                up, down = lax.rem(t + tiles - 1, tiles), lax.rem(t + 1, tiles)
                found.append(self.copy(self.su, self.rd, 6, 6, up, g))
                found.append(self.copy(self.sv, self.ru, 7, 7, down, g))
            elif name == "to_top":
                found.append(self.copy(self.sc, self.pc.at[t], 8, 10 + t, 0, west))
            elif name == "to_bottom":
                found.append(self.copy(self.sd, self.pd.at[t], 9, 10 + tiles + t, tiles - 1, west))
            for i in range(tiles):
                if name == "from_top":
                    found.append(self.copy(self.se.at[i], self.pe, 10 + i, 8, i, east))
                elif name == "from_bottom":
                    found.append(self.copy(self.sf.at[i], self.pf, 10 + tiles + i, 9, i, east))
                elif name == "at_top":
                    found.append(self.copy(self.sc, self.pc.at[i], 8, 10 + i, 0, west))
                elif name == "at_bottom":
                    found.append(self.copy(self.sd, self.pd.at[i], 9, 10 + tiles + i, 0, west))
        return found

    def start(self):
        tiles, w, rows, cols, x = self.tiles, self.width, self.rows, self.cols, self.x
        t = lax.axis_index("tile")
        own = pl.ds(w, rows)
        planes = [(q, k) for q in range(self.groups) for k in range(w)]
        inner = pl.ds(EDGE, cols)
        for q in range(self.groups):
            for f in range(3):
                self.su[q, f] = x[q, f, pl.ds(w, w), inner, :].astype(BF16)
                self.sv[q, f] = x[q, f, pl.ds(rows, w), inner, :].astype(BF16)
        for c in self.copies("rows"):
            c.start()
        first = [[x[q, f, own, EDGE + k, :] for q, k in planes] for f in range(3)]
        last = [[x[q, f, own, EDGE + cols - 1 - k, :] for q, k in planes] for f in range(3)]
        self.pack(self.sc, first[0])
        self.pack(self.sd, last[2])
        for c in self.copies("to_top", "to_bottom"):
            c.start()
        self.pack(self.sa, first[1] + first[2])
        self.pack(self.sb, last[0] + last[1])
        for c in self.copies("common"):
            c.start()

        def long(i, face, row_of):
            cells = pl.ds(EDGE + i * rows - w, rows + 2 * w)
            return [x[q, face, row_of(k), cells, :] for q, k in planes]

        @pl.when(t == 0)
        def _():
            for i, c in enumerate(self.copies("from_top")):
                self.pack(self.se.at[i], long(i, 0, lambda k: w + k))
                c.start()

        @pl.when(t == tiles - 1)
        def _():
            for i, c in enumerate(self.copies("from_bottom")):
                self.pack(self.sf.at[i], long(i, 2, lambda k: w + rows - 1 - k))
                c.start()

    def finish(self):
        tiles, w, rows, cols, x = self.tiles, self.width, self.rows, self.cols, self.x
        t = lax.axis_index("tile")
        for c in self.copies("common", "rows"):
            c.wait_recv()
        self.copy(self.se.at[0], self.pe, 10, 8, 0, 0).wait_recv()
        self.copy(self.sf.at[0], self.pf, 10, 9, 0, 0).wait_recv()
        planes = [(q, k) for q in range(self.groups) for k in range(w)]
        stage = self.stage
        for got, base, sign in ((self.rb, 1, -1), (self.ra, 0, 1)):
            for step in range(3):
                self.unpack(got.at[step])
                for f in range(2):
                    for n, (q, k) in enumerate(planes):
                        col = EDGE - 1 - k if sign < 0 else EDGE + cols + k
                        at = (f * len(planes) + n) * rows
                        if step == 0:
                            x[q, base + f, pl.ds(w + rows, w), col, :] = stage[pl.ds(at, w), :]
                        elif step == 1:
                            x[q, base + f, pl.ds(w, rows), col, :] = stage[pl.ds(at, rows), :]
                        else:
                            x[q, base + f, pl.ds(0, w), col, :] = stage[pl.ds(at + rows - w, w), :]
        for got, face, sign in ((self.pe, 0, -1), (self.pf, 2, 1)):
            self.unpack(got)
            for n, (q, k) in enumerate(planes):
                col = EDGE - 1 - k if sign < 0 else EDGE + cols + k
                x[q, face, :, col, :] = stage[pl.ds(n * (rows + 2 * w), rows + 2 * w), :]
        inner = pl.ds(EDGE, cols)
        for q in range(self.groups):
            for f in range(3):
                x[q, f, pl.ds(0, w), inner, :] = self.ru[q, f].astype(F32)
                x[q, f, pl.ds(w + rows, w), inner, :] = self.rd[q, f].astype(F32)
        blank = jnp.zeros((w, EDGE, LANES), F32)

        def no_corners(q, at):
            for f in range(3):
                x[q, f, pl.ds(at, w), pl.ds(0, EDGE), :] = blank
                x[q, f, pl.ds(at, w), pl.ds(EDGE + cols, EDGE), :] = blank

        def polar(name, packets, face, row_of):
            for i, c in enumerate(self.copies(name)):
                c.wait_recv()
                self.unpack(packets.at[i])
                for n, (q, k) in enumerate(planes):
                    x[q, face, row_of(k), pl.ds(EDGE + i * rows, rows), :] = stage[pl.ds(n * rows, rows), :]

        @pl.when(t == 0)
        def _():
            for q in range(self.groups):
                for f in range(2):
                    x[q, 1 + f, pl.ds(0, w), inner, :] = self.ru[q, f].astype(F32)
                no_corners(q, 0)
            polar("at_top", self.pc, 0, lambda k: w - 1 - k)

        @pl.when(t == tiles - 1)
        def _():
            for q in range(self.groups):
                for f in range(2):
                    x[q, f, pl.ds(w + rows, w), inner, :] = self.rd[q, 1 + f].astype(F32)
                no_corners(q, w + rows)
            polar("at_bottom", self.pd, 2, lambda k: w + rows + k)

    def drain(self):
        t = lax.axis_index("tile")
        for c in self.copies("common", "rows", "to_top", "to_bottom"):
            c.wait_send()

        @pl.when(t == 0)
        def _():
            for c in self.copies("from_top"):
                c.wait_send()

        @pl.when(t == self.tiles - 1)
        def _():
            for c in self.copies("from_bottom"):
                c.wait_send()


def blocks(rows, cols, body):
    if 3 * rows * cols <= 1024:
        body(0, 3, 0, rows)
        return
    height = max(1, min(rows, 512 // cols))
    per_face = rows // height

    @pl.loop(0, 3 * per_face)
    def _(i):
        body(i // per_face, 1, lax.rem(i, per_face) * height, height)


def conv_block(fields, weights, cols, dilation, face, faces, row, height):
    windows = []
    for tap in range(3):
        for field in fields:
            for q in range(field.shape[0]):
                got = field[q, pl.ds(face, faces), pl.ds(row, height + 2 * dilation),
                            pl.ds(EDGE + dilation * (tap - 1), cols), :]
                windows.append((tap, got.astype(BF16)))
    total = None
    for up in range(3):
        cut = [v[:, up * dilation : up * dilation + height].reshape(faces * height * cols, LANES)
               for _, v in windows]
        lhs = jnp.concatenate(cut, -1)
        rhs = weights[up]
        across = 0 if rhs.shape[0] == lhs.shape[1] else 1
        term = lax.dot_general(lhs, rhs, (((1,), (across,)), ((), ())), preferred_element_type=F32)
        total = term if total is None else total + term
    return total


def rounded(v):
    return v.astype(BF16).astype(F32)


def put(x, value, width, cols, face, faces, row, height):
    for q in range(x.shape[0]):
        part = value[:, q * LANES : (q + 1) * LANES].reshape(faces, height, cols, LANES)
        x[q, pl.ds(face, faces), pl.ds(width + row, height), pl.ds(EDGE, cols), :] = part


def get(x, width, cols, face, faces, row, height):
    parts = [
        x[q, pl.ds(face, faces), pl.ds(width + row, height), pl.ds(EDGE, cols), :].reshape(
            faces * height * cols, LANES)
        for q in range(x.shape[0])
    ]
    return jnp.concatenate(parts, -1) if len(parts) > 1 else parts[0]


def greet_first(tiles):
    t, g = lax.axis_index("tile"), lax.axis_index("face")
    faces = lax.axis_size("face")
    barrier = pltpu.get_barrier_semaphore()

    def signal(tile, face):
        pl.semaphore_signal(barrier, inc=1, device_id={"tile": tile, "face": face},
                            device_id_type=pl.DeviceIdType.MESH)

    for i in range(tiles):
        signal(i, lax.rem(g + 1, faces))
        signal(i, lax.rem(g + faces - 1, faces))
    signal(lax.rem(t + 1, tiles), g)
    signal(lax.rem(t + tiles - 1, tiles), g)


def greet_wait(tiles):
    pl.semaphore_wait(pltpu.get_barrier_semaphore(), 2 * tiles + 2)


def heighten(tall, weight, begin, size):
    outs = weight.shape[3]
    step = groups_of(size) * LANES
    tall[...] = jnp.zeros_like(tall)
    for up in range(3):
        for tap in range(3):
            tall[up, pl.ds(tap * step, size), pl.ds(0, outs)] = weight[up, tap, begin : begin + size, :]


def widen(wide, weight, parts):
    outs = weight.shape[2]
    step = sum(groups_of(size) for size in parts) * LANES
    wide[...] = jnp.zeros_like(wide)
    for up in range(3):
        for tap in range(3):
            at, begin = tap * step, 0
            for size in parts:
                wide[up, pl.ds(0, outs), pl.ds(at, size)] = weight[up, tap, :, begin : begin + size]
                at += groups_of(size) * LANES
                begin += size


def kernel(plans, tiles, state, *refs):
    far, (out, *scratch) = refs[:7], refs[7:]
    near, fetched = scratch[-8:-1], scratch[-1]
    scratch = scratch[:-8]
    fetches = [pltpu.make_async_copy(far[i], near[i], fetched.at[i]) for i in range(7)]
    w_in, w_block, w_mix, w_down, w_coarse, w_decode, w_out = near
    halos = []
    for i, plan in enumerate(plans):
        halos.append(Halo(scratch[FIELDS * i : FIELDS * i + FIELDS], *plan, tiles))
    wide, partial, k_in, k_block, k_mix, k_down, k_coarse, k_wide, k_skip, k_out = scratch[FIELDS * len(plans) :]
    source, encoded, skip, pooled, one, two = halos
    rows, cols = source.rows, source.cols
    c_rows, c_cols = pooled.rows, pooled.cols

    greet_first(tiles)
    for fetch in fetches:
        fetch.start()

    def first(*at):
        face, faces, row, height = at
        place = (0, pl.ds(face, faces), pl.ds(1 + row, height), pl.ds(EDGE, cols))
        source.x[place] = jnp.zeros((faces, height, cols, LANES), F32)
        for f in range(faces):
            for r in range(height):
                v = rounded(state[face + f, :, row + r, :]).T
                source.x[0, face + f, 1 + row + r, pl.ds(EDGE, cols), pl.ds(0, state.shape[1])] = v

    blocks(rows, cols, first)
    greet_wait(tiles)
    source.start()
    for fetch in fetches:
        fetch.wait()
    fields, c0, c1 = w_in.shape[2], w_block.shape[3], w_coarse.shape[3]
    heighten(k_in, w_in, 0, fields)
    widen(k_block, w_block, (c0,))
    k_mix[...] = jnp.zeros_like(k_mix)
    k_mix[pl.ds(0, c0), pl.ds(0, c0)] = w_mix[...]
    k_out[...] = jnp.zeros_like(k_out)
    k_out[:, pl.ds(0, c0)] = w_out[...]
    source.finish()

    def encode(*at):
        v = rounded(jax.nn.gelu(conv_block([source.x], k_in, cols, 1, *at)))
        put(encoded.x, v, 1, cols, *at)

    blocks(rows, cols, encode)
    encoded.start()
    widen(k_down, w_down, (c0,))
    widen(k_coarse, w_coarse, (c1,))
    heighten(k_wide, w_decode, 0, c1)
    heighten(k_skip, w_decode, c1, c0)
    encoded.finish()

    def block(*at):
        v = jax.nn.gelu(conv_block([encoded.x], k_block, cols, 1, *at)).astype(BF16)
        mixed = lax.dot_general(v, k_mix[...], (((1,), (1,)), ((), ())), preferred_element_type=F32)
        put(skip.x, rounded(get(encoded.x, 1, cols, *at) + mixed), 1, cols, *at)

    blocks(rows, cols, block)

    for f in range(3):
        for r in range(c_rows):
            total = None
            for i in range(2):
                for j in range(2):
                    v = skip.x[0, f, 1 + 2 * r + i, pl.ds(EDGE + j, c_cols, stride=2), :]
                    total = v if total is None else total + v
            pooled.x[0, f, 2 + r, pl.ds(EDGE, c_cols), :] = rounded(total * 0.25)
    pooled.start()
    skip.start()
    pooled.finish()

    def down(*at):
        v = rounded(jax.nn.gelu(conv_block([pooled.x], k_down, c_cols, 2, *at)))
        put(one.x, v, 1, c_cols, *at)

    blocks(c_rows, c_cols, down)
    one.start()
    one.finish()

    def coarse(*at):
        v = jax.nn.gelu(conv_block([one.x], k_coarse, c_cols, 1, *at))
        put(two.x, rounded(get(one.x, 1, c_cols, *at) + v), 1, c_cols, *at)

    blocks(c_rows, c_cols, coarse)
    two.start()
    skip.finish()

    def decode_skip(*at):
        put(partial, conv_block([skip.x], k_skip, cols, 1, *at), 0, cols, *at)

    blocks(rows, cols, decode_skip)
    two.finish()

    for q in range(wide.shape[0]):
        for f in range(3):
            for r in range(c_rows + 2):
                targets = [p for p in (2 * r - 1, 2 * r) if 0 <= p < rows + 2]
                v = two.x[q, f, r, pl.ds(EDGE, c_cols), :]
                rim_left = two.x[q, f, r, pl.ds(EDGE - 1, 1), :]
                rim_right = two.x[q, f, r, pl.ds(EDGE + c_cols, 1), :]
                for p in targets:
                    wide[q, f, p, pl.ds(EDGE, c_cols, stride=2), :] = v
                    wide[q, f, p, pl.ds(EDGE + 1, c_cols, stride=2), :] = v
                    wide[q, f, p, pl.ds(EDGE - 1, 1), :] = rim_left
                    wide[q, f, p, pl.ds(EDGE + cols, 1), :] = rim_right

    def decode(*at):
        face, faces, row, height = at
        total = get(partial, 0, cols, *at) + conv_block([wide], k_wide, cols, 1, *at)
        v = jax.nn.gelu(total).astype(BF16)
        read = lax.dot_general(k_out[...], v, (((1,), (1,)), ((), ())), preferred_element_type=F32)
        for f in range(faces):
            for r in range(height):
                at = (f * height + r) * cols
                out[face + f, :, row + r, :] = state[face + f, :, row + r, :] + read[:, at : at + cols]

    blocks(rows, cols, decode)
    for halo in halos:
        halo.drain()


def shards(atmosphere, weight_in, weight_block, weight_mix, weight_down, weight_coarse,
           weight_decode, readout_matrix):
    state = atmosphere[:, 0]
    _, fields, rows, cols = state.shape
    tiles = lax.axis_size("tile")
    c0, c1 = weight_block.shape[2], weight_down.shape[2]
    g0, g1 = groups_of(c0), groups_of(c1)
    plans = [
        (rows, cols, 1, 1),
        (rows, cols, 1, g0),
        (rows, cols, 1, g0),
        (rows // 2, cols // 2, 2, g0),
        (rows // 2, cols // 2, 1, g1),
        (rows // 2, cols // 2, 1, g1),
    ]
    scratch = [s for plan in plans for s in Halo.shapes(*plan, tiles)]
    scratch.append(pltpu.VMEM((g1, 3, rows + 2, cols + 2 * EDGE, LANES), F32))
    scratch.append(pltpu.VMEM((g0, 3, rows, cols + 2 * EDGE, LANES), F32))
    scratch += [
        pltpu.VMEM(s, BF16)
        for s in (
            (3, 3 * LANES, g0 * LANES),
            (3, g0 * LANES, 3 * g0 * LANES),
            (g0 * LANES, g0 * LANES),
            (3, g1 * LANES, 3 * g0 * LANES),
            (3, g1 * LANES, 3 * g1 * LANES),
            (3, 3 * g1 * LANES, g0 * LANES),
            (3, 3 * g0 * LANES, g0 * LANES),
            (fields, g0 * LANES),
        )
    ]
    weights = [jnp.swapaxes(weight_in, 2, 3), weight_block, weight_mix, weight_down, weight_coarse,
               jnp.swapaxes(weight_decode, 2, 3), readout_matrix]
    scratch += [pltpu.VMEM(v.shape, BF16) for v in weights]
    scratch.append(pltpu.SemaphoreType.DMA((len(weights),)))
    advanced = pl.pallas_call(
        functools.partial(kernel, plans, tiles),
        out_shape=jax.ShapeDtypeStruct((3, fields, rows, cols), F32),
        in_specs=[pl.BlockSpec(memory_space=pltpu.VMEM)] + [pl.BlockSpec(memory_space=pl.ANY)] * 7,
        out_specs=pl.BlockSpec(memory_space=pltpu.VMEM),
        scratch_shapes=scratch,
        compiler_params=pltpu.CompilerParams(
            collective_id=0, has_side_effects=True, vmem_limit_bytes=60 * 1024 * 1024),
    )(state, *weights)
    return advanced[:, None]


def solution(mesh):
    in_specs = (P("member", "face", None, "tile", None), P(), P(), P(), P(), P(), P(), P())
    out_specs = P("member", "face", None, "tile", None)
    return jax.shard_map(shards, mesh=mesh, in_specs=in_specs, out_specs=out_specs, check_vma=False)
```
